32 devices in a mesh: section: 2 (over x), dp: 4 (over y, core), expert: 4 (over z).
Axes of the slice: x: 2, y: 2, z: 4, core: 2. Of those that a mesh axis runs over, the one named last changes fastest.
Arguments:
- patches: bfloat16 [8192, 1152], P(('dp', 'expert')), may hold values from -50 to 50
- lengths: int32 [16, 4], P(('dp', 'expert')), may hold values from 1 to 64, 128 in all within a row
- w_qkv: bfloat16 [1152, 3456], P(None, 'section'), may hold values from -4.714045 to 4.714045
- w_out: bfloat16 [1152, 1152], P('section'), may hold values from -0.1875 to 0.1875
- w_proj: bfloat16 [4608, 2048], P('dp', 'section'), may hold values from -0.09375 to 0.09375
- routes: int32 [2048, 6], P(('dp', 'expert')), may hold values from 0 to 15, all different within a row; in each aligned block of 128 rows (0 to 127, 128 to 255, ...) at most 96 rows name the same one
- gates: float32 [2048, 6], P(('dp', 'expert')), may hold values from 0.05 to 0.4
- w_gate: bfloat16 [16, 2048, 1408], P(('dp', 'expert'), None, 'section'), may hold values from -0.125 to 0.125
- w_up: bfloat16 [16, 2048, 1408], P(('dp', 'expert'), None, 'section'), may hold values from -0.125 to 0.125
- w_down: bfloat16 [16, 1408, 2048], P(('dp', 'expert'), 'section'), may hold values from -0.15625 to 0.15625
Outputs:
- language_out: bfloat16 [2048, 2048], P(('dp', 'expert'), 'section')
The draws below stay inside these ranges and needn't reach their ends.
Inputs may be any that keep to these rules, and one draw needn't show every extreme that they name: Each row lists, in order, the lengths in merged tokens of a group's images; they sum to 128 and the largest is exactly 64. `routes`: A token's 6 experts differ. Among the rows of one device no expert is named more than 96 times, a bound that some block reaches in every draw.
All inputs are finite; a program needn't handle non-finite values.
Results may differ from the reference program's by a relative error of at most 0.012.
Values may be sent and summed in bfloat16 or wider, within the bound.
A program may use at most 64 MiB of HBM per device.

```python
import math
import jax
import jax.numpy as jnp
import numpy as np
from jax import lax

D_VIT = 1152
HEADS = 16
D_LM = 2048
FF_EXP = 1408
TOP = 6
IMAGES = 4
GROUPS = 16
EXPERTS = 16
M_DEV = 128
PATCHES = 8192
TOKENS = 2048
CAP = 96
N_SECTION = 2


def draw_patches(key, part):
    keys = jax.random.split(key, 4)
    columns = jnp.exp(jax.random.uniform(keys[0], (D_VIT,), jnp.float32) * math.log(10.0))
    offsets = jax.random.uniform(keys[2], (D_VIT,), jnp.float32, -1.0, 1.0)
    noise = jnp.clip(jax.random.normal(keys[3], (PATCHES, D_VIT), jnp.float32), -4.0, 4.0)
    row_scale = jnp.exp(jax.random.uniform(keys[1], (PATCHES, 1), jnp.float32) * math.log(10.0)) * 0.1
    return ((noise + offsets[None, :]) * columns[None, :] * row_scale).astype(jnp.bfloat16)


def draw_w_qkv(key, part):
    keys = jax.random.split(key, 1)
    head_dim = D_VIT // HEADS
    raw = jnp.clip(jax.random.normal(keys[0], (D_VIT, HEADS, 3, head_dim), jnp.float32), -4.0, 4.0)
    raw = raw * (1.0 / math.sqrt(D_VIT))
    return raw.reshape(D_VIT, 3 * D_VIT).astype(jnp.bfloat16)


def block_levels(stream_key, dims, pieces, low, top_value):
    factor_of = 1.0
    for dim, parts in pieces:
        heights = jax.random.uniform(jax.random.fold_in(jax.random.fold_in(stream_key, 6), dim), (parts,), jnp.float32, low / len(pieces), top_value / len(pieces))
        factor_of = factor_of * jnp.repeat(jnp.exp(heights), dims[dim] // parts).reshape((-1,) + (1,) * (len(dims) - 1 - dim))
    return factor_of


def split_up(amount, total, most, lean):
    portions = [(1 << 20) // math.isqrt(standing ** lean) + 1 for standing in range(2, amount + 1)]
    surplus, given = total - most - (amount - 1), [1] * (amount - 1)
    while surplus > 0:
        candidates = [i for i in range(amount - 1) if given[i] < most]
        whole, budget = sum([portions[i] for i in candidates]), surplus
        for i in candidates:
            extra = min(most - given[i], max(1, budget * portions[i] // whole), surplus)
            given[i] = given[i] + extra
            surplus = surplus - extra
    return np.array([most] + given)


def ragged(key, number_of, total, limit, lean):
    if number_of == 2:
        one = jax.random.randint(key, (), max(1, total - limit), min(limit, total - 1) + 1)
        return jnp.stack([one, total - one])
    sizes = jnp.asarray(split_up(number_of, total, limit, lean), jnp.int32)
    couples = (number_of - 1) // 2
    source_of, sink = sizes[1:1 + 2 * couples:2], sizes[2:2 + 2 * couples:2]
    room = jnp.minimum(source_of - 1, limit - sink)
    passed = jax.random.randint(jax.random.fold_in(key, 1), (couples,), 0, 1 << 20) % (room + 1)
    sizes = sizes.at[1:1 + 2 * couples:2].set(source_of - passed).at[2:2 + 2 * couples:2].set(sink + passed)
    return sizes[jax.random.permutation(jax.random.fold_in(key, 2), number_of)]


def assign_block(rng, own, number, rows, amount, top, reach, skew):
    sequence = jax.random.permutation(rng, amount)
    crowded, usual = load_shares(amount, rows * top, reach, skew, True), load_shares(amount, rows * top, reach, skew, False)
    places = jnp.arange(amount)

    def named(sizes, turn):
        used = int((sizes > 0).sum())
        fixed = max(1, used // 4)
        passed = fixed + (places - fixed + turn * (used - fixed)) % max(1, amount - fixed)
        return jnp.zeros((amount,), jnp.int32).at[sequence[jnp.where(places < fixed, places, passed)]].set(jnp.asarray(sizes, jnp.int32))

    sizes = jnp.where(number % 4 == 0, named(crowded, number // 4), named(usual, number - number // 4 - 1))
    mixed = jax.random.permutation(jax.random.fold_in(own, 3), amount)
    source_of, sink = mixed[0:amount // 2 * 2:2], mixed[1:amount // 2 * 2:2]
    margin = jnp.minimum(sizes[source_of] - 1, reach - sizes[sink]) // 2
    margin = jnp.where((source_of == sequence[0]) | (sink == sequence[0]) | (sizes[sink] == 0), 0, jnp.maximum(margin, 0))
    passed = jax.random.randint(jax.random.fold_in(own, 4), (amount // 2,), 0, 1 << 20) % (margin + 1)
    sizes = sizes.at[source_of].add(-passed).at[sink].add(passed)
    labels = jnp.searchsorted(jnp.cumsum(sizes), jnp.arange(rows * top), side="right").astype(jnp.int32)
    table = labels.reshape(top, rows).T
    table = table[jax.random.permutation(jax.random.fold_in(own, 1), rows)]
    turn = jax.random.randint(jax.random.fold_in(own, 2), (rows, 1), 0, top)
    return jnp.take_along_axis(table, (jnp.arange(top)[None, :] + turn) % top, axis=1)


def load_shares(number_of, total, reach, skew, full):
    loads = [(1 << 20) // math.isqrt(rank ** skew) + 1 for rank in range(1, number_of + 1)]
    largest = reach if full else min(reach, max(-(-total // number_of), total * loads[0] // sum(loads)))
    least = 1 if total - largest >= number_of - 1 else 0
    given, spare = [largest] + [least] * (number_of - 1), total - largest - least * (number_of - 1)
    while spare > 0:
        free = [i for i in range(1, number_of) if given[i] < largest] or [i for i in range(1, number_of) if given[i] < reach]
        pool, left = sum([loads[i] for i in free]), spare
        for i in free:
            addition = min(reach - given[i], max(1, left * loads[i] // pool), spare)
            given[i] = given[i] + addition
            spare = spare - addition
    return np.array(given)


def bell_draw(stream_key, extent, width, most, pieces=(), held_as=jnp.bfloat16):
    values = jax.random.normal(stream_key, extent, jnp.float32) * width
    if len(pieces) > 0:
        values = block_levels(stream_key, extent, pieces, -0.22, 0.18) * values
    return jnp.clip(values, min=-most, max=most).astype(held_as)


def setup_inputs(seed: int = 0) -> dict:
    arg_keys = jax.random.split(jax.random.key(seed), 11)
    patches = draw_patches(jax.random.fold_in(arg_keys[10], 71), 0)
    lengths = jax.vmap(lambda own: ragged(own, IMAGES, M_DEV, M_DEV // 2, 2))(jax.random.split(arg_keys[1], GROUPS)).reshape((GROUPS, IMAGES)).astype(jnp.int32)
    w_qkv = draw_w_qkv(jax.random.fold_in(arg_keys[10], 71), 0)
    w_out = bell_draw(arg_keys[3], (D_VIT, D_VIT), D_VIT ** -0.5, 0.1875, ((0, 2),))
    w_proj = bell_draw(arg_keys[4], (4 * D_VIT, D_LM), (4 * D_VIT) ** -0.5, 0.09375, ((0, 4), (1, 2)))
    routes_keys = jax.random.split(jax.random.fold_in(arg_keys[5], 1), TOKENS // M_DEV)
    routes_turns = jax.random.permutation(jax.random.fold_in(arg_keys[5], 3), TOKENS // M_DEV)
    routes = jax.vmap(lambda own, number: assign_block(jax.random.fold_in(arg_keys[5], 2), own, number, M_DEV, EXPERTS, TOP, CAP, 2))(routes_keys, routes_turns).reshape((TOKENS, TOP))
    gates = jnp.clip(0.05 + 0.35 * jax.random.uniform(arg_keys[6], (TOKENS, TOP), jnp.float32) ** block_levels(arg_keys[6], (TOKENS, TOP), ((0, 16),), -0.2, 0.2), 0.05, 0.4)
    w_gate = bell_draw(arg_keys[7], (EXPERTS, D_LM, FF_EXP), D_LM ** -0.5, 0.125, ((0, 16), (2, 2)))
    w_up = bell_draw(arg_keys[8], (EXPERTS, D_LM, FF_EXP), D_LM ** -0.5, 0.125, ((0, 16), (2, 2)))
    w_down = bell_draw(arg_keys[9], (EXPERTS, FF_EXP, D_LM), FF_EXP ** -0.5, 0.15625, ((0, 16), (1, 2)))
    return {"patches": patches, "lengths": lengths, "w_qkv": w_qkv, "w_out": w_out, "w_proj": w_proj, "routes": routes, "gates": gates, "w_gate": w_gate, "w_up": w_up, "w_down": w_down}


def layer_norm(values):
    center = values - lax.optimization_barrier(jnp.mean(values, axis=-1, keepdims=True))
    spread = lax.optimization_barrier(jnp.mean(center * center, axis=-1, keepdims=True))
    return center * lax.rsqrt(spread + 1e-06)

def rms_norm(values):
    return values * lax.rsqrt(lax.optimization_barrier(jnp.mean(values * values, axis=-1, keepdims=True)) + 1e-06)

def segment_of(lengths_row, patch_count):
    ends = jnp.cumsum(lengths_row).astype(jnp.int32) * 4
    places = jnp.arange(patch_count, dtype=jnp.int32)
    return lax.optimization_barrier(jnp.sum((places[:, None] >= ends[None, :]).astype(jnp.int32), axis=1))

def reference(patches, lengths, w_qkv, w_out, w_proj, routes, gates, w_gate, w_up, w_down):
    groups = lengths.shape[0]
    patch_rows = patches.shape[0] // groups
    head_dim = D_VIT // HEADS
    scale = 1.0 / math.sqrt(head_dim)

    def encode(blocks):
        inputs, lengths_row = blocks
        normed_in = layer_norm(inputs.astype(jnp.float32)).astype(jnp.bfloat16)
        packed = jnp.dot(normed_in, w_qkv, preferred_element_type=jnp.float32).astype(jnp.bfloat16)
        packed = packed.reshape(patch_rows, HEADS, 3, head_dim).astype(jnp.float32)
        query = packed[:, :, 0]
        key_part = packed[:, :, 1]
        value_part = packed[:, :, 2]
        segment = segment_of(lengths_row, patch_rows)
        same = segment[:, None] == segment[None, :]
        scores = jnp.einsum('qhd,khd->hqk', query, key_part) * scale
        scores = jnp.where(same[None], scores, -jnp.inf)
        peak = lax.optimization_barrier(jnp.max(scores, axis=-1, keepdims=True))
        weights = jnp.where(same[None], jnp.exp(scores - peak), 0.0)
        probs = (weights / lax.optimization_barrier(jnp.sum(weights, axis=-1, keepdims=True))).astype(jnp.bfloat16)
        attended = jnp.einsum('hqk,khd->qhd', probs.astype(jnp.float32), value_part).astype(jnp.bfloat16)
        mixed = jnp.dot(attended.reshape(patch_rows, D_VIT), w_out, preferred_element_type=jnp.float32)
        encoded = inputs.astype(jnp.float32) + mixed
        return encoded.reshape(patch_rows // 4, 4 * D_VIT).astype(jnp.bfloat16)
    merged = lax.map(encode, (patches.reshape(groups, patch_rows, D_VIT), lengths))
    merged = merged.reshape(-1, 4 * D_VIT)
    projected = jnp.dot(merged, w_proj, preferred_element_type=jnp.float32).astype(jnp.bfloat16)
    normed_tokens = rms_norm(projected.astype(jnp.float32)).astype(jnp.bfloat16)
    token_total = projected.shape[0]
    merged_count = token_total // groups
    route_flat = routes.reshape(groups, merged_count * TOP)
    onehot = (route_flat[:, :, None] == jnp.arange(EXPERTS, dtype=jnp.int32)[None, None, :]).astype(jnp.int32)
    ranks = jnp.cumsum(onehot, axis=1).astype(jnp.int32) - 1
    slots = lax.optimization_barrier(jnp.sum(ranks * onehot, axis=2)).astype(jnp.int32)
    group_index = jnp.arange(groups, dtype=jnp.int32)[:, None]
    owners = group_index * merged_count + jnp.arange(merged_count * TOP, dtype=jnp.int32)[None, :] // TOP
    places = group_index * CAP + slots
    table = jnp.full((EXPERTS, groups * CAP), token_total, dtype=jnp.int32).at[route_flat, places].set(owners.astype(jnp.int32))
    weight_table = jnp.zeros((EXPERTS, groups * CAP), dtype=jnp.float32).at[route_flat, places].set(gates.reshape(groups, merged_count * TOP))
    padded = jnp.concatenate([normed_tokens, jnp.zeros((1, D_LM), dtype=jnp.bfloat16)], axis=0)
    quarter = FF_EXP // N_SECTION

    def expert_step(total, expert_index):
        picked = padded[table[expert_index]]
        gate_act = jnp.dot(picked, w_gate[expert_index], preferred_element_type=jnp.float32)
        up_act = jnp.dot(picked, w_up[expert_index], preferred_element_type=jnp.float32)
        hidden = (jax.nn.silu(gate_act) * up_act).astype(jnp.bfloat16)
        result = jnp.zeros((picked.shape[0], D_LM), dtype=jnp.float32)
        for quarter_index in range(N_SECTION):
            lower = quarter_index * quarter
            piece = jnp.dot(hidden[:, lower:lower + quarter], w_down[expert_index, lower:lower + quarter], preferred_element_type=jnp.float32).astype(jnp.bfloat16)
            piece = lax.optimization_barrier(piece)
            result = result + piece.astype(jnp.float32)
        total = total.at[table[expert_index]].add(weight_table[expert_index][:, None] * result)
        return (total, None)
    start_total = jnp.zeros((token_total + 1, D_LM), dtype=jnp.float32)
    expert_sum, unused = lax.scan(expert_step, start_total, jnp.arange(EXPERTS, dtype=jnp.int32))
    return (projected.astype(jnp.float32) + expert_sum[:token_total]).astype(jnp.bfloat16)
```

```python
import math

import jax
import jax.numpy as jnp
from jax import lax
from jax.sharding import PartitionSpec as P

D_VIT = 1152
HEADS = 16
TOP = 6


def layer_norm(values):
    center = values - jnp.mean(values, axis=-1, keepdims=True)
    spread = jnp.mean(center * center, axis=-1, keepdims=True)
    return center * lax.rsqrt(spread + 1e-06)


def rms_norm(values):
    return values * lax.rsqrt(jnp.mean(values * values, axis=-1, keepdims=True) + 1e-06)


def dense_experts(proj_own, routes, gates, w_gate, w_up, w_down):
    everyone = ("dp", "expert", "section")
    sections = lax.axis_size("section")
    groups = lax.axis_size("dp") * lax.axis_size("expert")
    rows, part = proj_own.shape
    own_expert = lax.axis_index("dp") * lax.axis_size("expert") + lax.axis_index("expert")
    per_expert = jnp.sum(
        jnp.where(
            routes[:, :, None] == jnp.arange(groups, dtype=jnp.int32)[None, None, :],
            gates[:, :, None],
            0.0,
        ),
        axis=1,
    )
    weight = lax.all_gather(per_expert, ("dp", "expert"), axis=0, tiled=True)
    weight = jnp.sum(
        jnp.where(jnp.arange(groups, dtype=jnp.int32)[None, :] == own_expert, weight, 0.0),
        axis=1,
        keepdims=True,
    )
    tokens = lax.all_gather(proj_own, everyone, axis=0, tiled=False)
    tokens = tokens.reshape(groups, sections, rows, part)
    pieces = [tokens[:, q].reshape(groups * rows, part) for q in range(sections)]
    squares = sum(
        jnp.sum(jnp.square(piece.astype(jnp.float32)), axis=1, keepdims=True) for piece in pieces
    )
    inverse = lax.rsqrt(squares / (sections * part) + 1e-06)
    gate_act = sum(
        jnp.dot(
            piece, w_gate[0, q * part : (q + 1) * part], preferred_element_type=jnp.float32
        )
        for q, piece in enumerate(pieces)
    )
    up_act = sum(
        jnp.dot(piece, w_up[0, q * part : (q + 1) * part], preferred_element_type=jnp.float32)
        for q, piece in enumerate(pieces)
    )
    hidden = (jax.nn.silu(gate_act * inverse) * (up_act * inverse)).astype(jnp.bfloat16)
    sums = [
        (
            jnp.dot(
                hidden, w_down[0, :, q * part : (q + 1) * part], preferred_element_type=jnp.float32
            )
            * weight
        )
        .astype(jnp.bfloat16)
        .reshape(groups, rows, part)
        for q in range(sections)
    ]
    shares = jnp.stack(sums, axis=1).reshape(groups * sections * rows, part)
    total = lax.psum_scatter(shares, everyone, scatter_dimension=0, tiled=True)
    return (proj_own.astype(jnp.float32) + total.astype(jnp.float32)).astype(jnp.bfloat16)


def routed_experts(proj_own, routes, gates, w_gate, w_up, w_down, capacity):
    projected = lax.all_gather(proj_own, "section", axis=1, tiled=True)
    model_width = projected.shape[1]
    normed_tokens = rms_norm(projected.astype(jnp.float32)).astype(jnp.bfloat16)
    expert_total = lax.axis_size("dp") * lax.axis_size("expert")
    merged_count = proj_own.shape[0]
    route_flat = routes.reshape(-1)
    onehot = (route_flat[:, None] == jnp.arange(expert_total, dtype=jnp.int32)[None, :]).astype(
        jnp.int32
    )
    ranks = jnp.cumsum(onehot, axis=0) - 1
    slots = jnp.sum(ranks * onehot, axis=1)
    target = route_flat * capacity + slots
    owners = jnp.arange(merged_count * TOP, dtype=jnp.int32) // TOP
    source = jnp.zeros((expert_total * capacity,), dtype=jnp.int32).at[target].set(owners)
    outgoing = normed_tokens[source].reshape(expert_total, capacity, model_width)
    received = lax.all_to_all(outgoing, ("dp", "expert"), split_axis=0, concat_axis=0, tiled=True)
    flat_rows = received.reshape(-1, received.shape[-1])
    gate_act = jnp.dot(flat_rows, w_gate[0], preferred_element_type=jnp.float32)
    up_act = jnp.dot(flat_rows, w_up[0], preferred_element_type=jnp.float32)
    hidden = (jax.nn.silu(gate_act) * up_act).astype(jnp.bfloat16)
    result = jnp.dot(hidden, w_down[0], preferred_element_type=jnp.float32).astype(jnp.bfloat16)
    returned = lax.all_to_all(
        result.reshape(received.shape[:-1] + (w_down.shape[2],)),
        ("dp", "expert"),
        split_axis=0,
        concat_axis=0,
        tiled=True,
    )
    picked = returned.reshape(expert_total * capacity, model_width)[target].reshape(
        merged_count, TOP, model_width
    )
    weighted = jnp.zeros((merged_count, model_width), dtype=jnp.float32)
    for choice_index in range(TOP):
        weighted = weighted + gates[:, choice_index : choice_index + 1] * picked[
            :, choice_index
        ].astype(jnp.float32)
    expert_cols = lax.psum_scatter(
        weighted.astype(jnp.bfloat16), "section", scatter_dimension=1, tiled=True
    ).astype(jnp.float32)
    return (proj_own.astype(jnp.float32) + expert_cols).astype(jnp.bfloat16)


def per_device(patches, lengths, w_qkv, w_out, w_proj, routes, gates, w_gate, w_up, w_down):
    data_count = lax.axis_size("dp")
    owner_count = lax.axis_size("expert")
    patch_rows, width = patches.shape
    head_dim = D_VIT // HEADS
    local_heads = w_qkv.shape[1] // (3 * head_dim)
    scale = 1.0 / math.sqrt(head_dim)
    normed_in = layer_norm(patches.astype(jnp.float32)).astype(jnp.bfloat16)
    packed = jnp.dot(normed_in, w_qkv, preferred_element_type=jnp.float32).astype(jnp.bfloat16)
    packed = packed.reshape(patch_rows, local_heads, 3, head_dim)
    query = packed[:, :, 0]
    key_part = packed[:, :, 1]
    value_part = packed[:, :, 2]
    ends = jnp.cumsum(lengths[0]) * 4
    places = jnp.arange(patch_rows, dtype=jnp.int32)
    segment = jnp.sum((places[:, None] >= ends[None, :]).astype(jnp.int32), axis=1)
    block_rows = min(patch_rows, 512)
    block_count = patch_rows // block_rows

    def attend(blocks):
        query_block, segment_block = blocks
        scores = (
            jnp.einsum("qhd,khd->hqk", query_block, key_part, preferred_element_type=jnp.float32)
            * scale
        )
        same = segment_block[:, None] == segment[None, :]
        scores = jnp.where(same[None], scores, -jnp.inf)
        peak = jnp.max(scores, axis=-1, keepdims=True)
        weights = jnp.where(same[None], jnp.exp(scores - peak), 0.0)
        probs = (weights / jnp.sum(weights, axis=-1, keepdims=True)).astype(jnp.bfloat16)
        result = jnp.einsum("hqk,khd->qhd", probs, value_part, preferred_element_type=jnp.float32)
        return result.astype(jnp.bfloat16).reshape(block_rows, local_heads * head_dim)

    attended = lax.map(
        attend,
        (
            query.reshape(block_count, block_rows, local_heads, head_dim),
            segment.reshape(block_count, block_rows),
        ),
    )
    attended = attended.reshape(patch_rows, local_heads * head_dim)
    merged_count = patch_rows // 4
    summed = lax.psum(
        jnp.dot(attended, w_out, preferred_element_type=jnp.float32).astype(jnp.bfloat16), "section"
    ).astype(jnp.float32)
    merged = (
        (patches.astype(jnp.float32) + summed).reshape(merged_count, 4 * width).astype(jnp.bfloat16)
    )
    proj_own = jnp.dot(
        merged, lax.all_gather(w_proj, "dp", axis=0, tiled=True), preferred_element_type=jnp.float32
    ).astype(jnp.bfloat16)
    expert_total = data_count * owner_count
    capacity = max(2, min(merged_count, 2 * merged_count * TOP // expert_total))
    if merged_count <= 2 * capacity:
        return dense_experts(proj_own, routes, gates, w_gate, w_up, w_down)
    return routed_experts(proj_own, routes, gates, w_gate, w_up, w_down, capacity)


def solution(mesh):
    return jax.shard_map(
        per_device,
        mesh=mesh,
        in_specs=(
            P(("dp", "expert"), None),
            P(("dp", "expert"), None),
            P(None, "section"),
            P("section", None),
            P("dp", "section"),
            P(("dp", "expert"), None),
            P(("dp", "expert"), None),
            P(("dp", "expert"), None, "section"),
            P(("dp", "expert"), None, "section"),
            P(("dp", "expert"), "section", None),
        ),
        out_specs=P(("dp", "expert"), "section"),
        check_vma=False,
    )
```

```python
import math

import jax
import jax.numpy as jnp
from jax import lax
from jax.sharding import PartitionSpec as P

D_VIT = 1152
HEADS = 16
TOP = 6


def layer_norm(values):
    center = values - jnp.mean(values, axis=-1, keepdims=True)
    spread = jnp.mean(center * center, axis=-1, keepdims=True)
    return center * lax.rsqrt(spread + 1e-06)


def rms_norm(values):
    return values * lax.rsqrt(jnp.mean(values * values, axis=-1, keepdims=True) + 1e-06)


def swapped(values, axis, bit):
    count = lax.axis_size(axis)
    return lax.ppermute(values, axis, [(i, i ^ bit) for i in range(count)])


def halves(values):
    high = lax.reduce_precision(values, 8, 7)
    return [high.astype(jnp.bfloat16), (values - high).astype(jnp.bfloat16)]


def pair_sum(own, other):
    return (own.astype(jnp.float32) + other.astype(jnp.float32)).astype(jnp.bfloat16)


def pick(values, index, axis):
    return lax.dynamic_index_in_dim(values, index, axis, keepdims=False)


def dense_experts(proj_own, routes, gates, w_gate, w_up, w_down):
    sections = lax.axis_size("section")
    data_count = lax.axis_size("dp")
    owners = lax.axis_size("expert")
    groups = data_count * owners
    rows, part = proj_own.shape
    me_d, me_e, me_s = lax.axis_index("dp"), lax.axis_index("expert"), lax.axis_index("section")
    per_expert = jnp.sum(
        jnp.where(
            routes[:, :, None] == jnp.arange(groups, dtype=jnp.int32)[None, None, :],
            gates[:, :, None],
            0.0,
        ),
        axis=1,
    )
    own = proj_own.astype(jnp.float32)
    side = halves(per_expert) + halves(jnp.sum(own * own, axis=1, keepdims=True))
    side = jnp.concatenate(side, axis=1)
    side_width = -(-side.shape[1] // 128) * 128
    side = jnp.pad(side, ((0, 0), (0, side_width - side.shape[1])))
    sent = jnp.concatenate([proj_own, side], axis=1)
    gathered = lax.all_gather(sent, ("dp", "expert", "section"), axis=0, tiled=False)
    gathered = gathered.reshape(data_count, owners, sections, rows, part + side_width)
    down = [
        lax.dynamic_slice_in_dim(w_down[0], (me_s ^ flip) * part, part, axis=1)
        for flip in range(sections)
    ]
    own_expert = me_d * owners + me_e
    at_expert = jnp.arange(groups, dtype=jnp.int32)[None, :] == own_expert

    def run(flip_d):
        block = pick(gathered, me_d ^ flip_d, 0)
        block = [block[:, q].reshape(owners * rows, part + side_width) for q in range(sections)]
        tokens = [piece[:, :part] for piece in block]
        sides = [piece[:, part:].astype(jnp.float32) for piece in block]
        weight = sides[0][:, :groups] + sides[0][:, groups : 2 * groups]
        weight = jnp.sum(jnp.where(at_expert, weight, 0.0), axis=1, keepdims=True)
        squares = sum(
            piece[:, 2 * groups : 2 * groups + 1] + piece[:, 2 * groups + 1 : 2 * groups + 2]
            for piece in sides
        )
        inverse = lax.rsqrt(squares / (sections * part) + 1e-06)

        def through(matrix):
            product = sum(
                jnp.dot(
                    piece,
                    matrix[0, q * part : (q + 1) * part],
                    preferred_element_type=jnp.float32,
                )
                for q, piece in enumerate(tokens)
            )
            return product * inverse

        hidden = (jax.nn.silu(through(w_gate)) * through(w_up)).astype(jnp.bfloat16)
        return [
            (jnp.dot(hidden, piece, preferred_element_type=jnp.float32) * weight).astype(
                jnp.bfloat16
            )
            for piece in down
        ]

    partial = {flip: run(flip) for flip in sorted(range(data_count), key=lambda f: (-(f & 1), -f))}
    near = {}
    for flip in range(data_count - 2, -1, -2):
        near[flip] = [
            pair_sum(partial[flip][q], swapped(partial[flip + 1][q], "dp", 1))
            for q in range(sections)
        ]
    half = part // 2
    left = [piece[:, :half] for piece in near[0]], [piece[:, :half] for piece in near[2]]
    right = [piece[:, half:] for piece in near[0]], [piece[:, half:] for piece in near[2]]
    far_left = pair_sum(left[1][0], swapped(left[1][1], "section", 1))
    far_right = pair_sum(right[0][1], swapped(right[1][1], "dp", 2))
    mid_left = pair_sum(left[0][0], swapped(left[0][1], "section", 1))
    mid_right = pair_sum(right[0][0], swapped(right[1][0], "dp", 2))
    mid_left = pair_sum(mid_left, swapped(far_left, "dp", 2))
    mid_right = pair_sum(mid_right, swapped(far_right, "section", 1))
    ends = []
    for piece in (mid_left, mid_right):
        piece = piece.reshape(owners // 2, 2, rows, half)
        low = me_e & 1
        piece = pair_sum(pick(piece, low, 1), swapped(pick(piece, 1 - low, 1), "expert", 1))
        high = me_e // 2
        ends.append(
            pick(piece, high, 0).astype(jnp.float32)
            + swapped(pick(piece, 1 - high, 0), "expert", 2).astype(jnp.float32)
        )
    return (own + jnp.concatenate(ends, axis=1)).astype(jnp.bfloat16)


def routed_experts(proj_own, routes, gates, w_gate, w_up, w_down, capacity):
    projected = lax.all_gather(proj_own, "section", axis=1, tiled=True)
    model_width = projected.shape[1]
    normed_tokens = rms_norm(projected.astype(jnp.float32)).astype(jnp.bfloat16)
    expert_total = lax.axis_size("dp") * lax.axis_size("expert")
    merged_count = proj_own.shape[0]
    route_flat = routes.reshape(-1)
    onehot = (route_flat[:, None] == jnp.arange(expert_total, dtype=jnp.int32)[None, :]).astype(
        jnp.int32
    )
    ranks = jnp.cumsum(onehot, axis=0) - 1
    slots = jnp.sum(ranks * onehot, axis=1)
    target = route_flat * capacity + slots
    owners = jnp.arange(merged_count * TOP, dtype=jnp.int32) // TOP
    source = jnp.zeros((expert_total * capacity,), dtype=jnp.int32).at[target].set(owners)
    outgoing = normed_tokens[source].reshape(expert_total, capacity, model_width)
    received = lax.all_to_all(outgoing, ("dp", "expert"), split_axis=0, concat_axis=0, tiled=True)
    flat_rows = received.reshape(-1, received.shape[-1])
    gate_act = jnp.dot(flat_rows, w_gate[0], preferred_element_type=jnp.float32)
    up_act = jnp.dot(flat_rows, w_up[0], preferred_element_type=jnp.float32)
    hidden = (jax.nn.silu(gate_act) * up_act).astype(jnp.bfloat16)
    result = jnp.dot(hidden, w_down[0], preferred_element_type=jnp.float32).astype(jnp.bfloat16)
    returned = lax.all_to_all(
        result.reshape(received.shape[:-1] + (w_down.shape[2],)),
        ("dp", "expert"),
        split_axis=0,
        concat_axis=0,
        tiled=True,
    )
    picked = returned.reshape(expert_total * capacity, model_width)[target].reshape(
        merged_count, TOP, model_width
    )
    weighted = jnp.zeros((merged_count, model_width), dtype=jnp.float32)
    for choice_index in range(TOP):
        weighted = weighted + gates[:, choice_index : choice_index + 1] * picked[
            :, choice_index
        ].astype(jnp.float32)
    expert_cols = lax.psum_scatter(
        weighted.astype(jnp.bfloat16), "section", scatter_dimension=1, tiled=True
    ).astype(jnp.float32)
    return (proj_own.astype(jnp.float32) + expert_cols).astype(jnp.bfloat16)


def per_device(patches, lengths, w_qkv, w_out, w_proj, routes, gates, w_gate, w_up, w_down):
    data_count = lax.axis_size("dp")
    owner_count = lax.axis_size("expert")
    patch_rows, width = patches.shape
    head_dim = D_VIT // HEADS
    local_heads = w_qkv.shape[1] // (3 * head_dim)
    scale = 1.0 / math.sqrt(head_dim)
    shards = [(0, w_proj)]
    bit = data_count // 2
    while bit >= 1:
        shards = shards + [(flip ^ bit, swapped(shard, "dp", bit)) for flip, shard in shards]
        bit //= 2
    normed_in = layer_norm(patches.astype(jnp.float32)).astype(jnp.bfloat16)
    packed = jnp.dot(normed_in, w_qkv, preferred_element_type=jnp.float32).astype(jnp.bfloat16)
    packed = packed.reshape(patch_rows, local_heads, 3, head_dim)
    query = packed[:, :, 0]
    key_part = packed[:, :, 1]
    value_part = packed[:, :, 2]
    ends = jnp.cumsum(lengths[0]) * 4
    places = jnp.arange(patch_rows, dtype=jnp.int32)
    segment = jnp.sum((places[:, None] >= ends[None, :]).astype(jnp.int32), axis=1)
    block_rows = min(patch_rows, 512)
    block_count = patch_rows // block_rows

    def attend(blocks):
        query_block, segment_block = blocks
        scores = (
            jnp.einsum("qhd,khd->hqk", query_block, key_part, preferred_element_type=jnp.float32)
            * scale
        )
        same = segment_block[:, None] == segment[None, :]
        scores = jnp.where(same[None], scores, -jnp.inf)
        peak = jnp.max(scores, axis=-1, keepdims=True)
        weights = jnp.where(same[None], jnp.exp(scores - peak), 0.0)
        probs = (weights / jnp.sum(weights, axis=-1, keepdims=True)).astype(jnp.bfloat16)
        result = jnp.einsum("hqk,khd->qhd", probs, value_part, preferred_element_type=jnp.float32)
        return result.astype(jnp.bfloat16).reshape(block_rows, local_heads * head_dim)

    attended = lax.map(
        attend,
        (
            query.reshape(block_count, block_rows, local_heads, head_dim),
            segment.reshape(block_count, block_rows),
        ),
    )
    attended = attended.reshape(patch_rows, local_heads * head_dim)
    merged_count = patch_rows // 4
    mixed = jnp.dot(attended, w_out, preferred_element_type=jnp.float32).astype(jnp.bfloat16)
    if lax.axis_size("section") == 2:
        summed = mixed.astype(jnp.float32) + swapped(mixed, "section", 1).astype(jnp.float32)
    else:
        summed = lax.psum(mixed, "section").astype(jnp.float32)
    merged = (
        (patches.astype(jnp.float32) + summed).reshape(merged_count, 4 * width).astype(jnp.bfloat16)
    )
    depth = w_proj.shape[0]
    me_d = lax.axis_index("dp")
    proj_own = sum(
        jnp.dot(
            lax.dynamic_slice_in_dim(merged, (me_d ^ flip) * depth, depth, axis=1),
            shard,
            preferred_element_type=jnp.float32,
        )
        for flip, shard in shards
    ).astype(jnp.bfloat16)
    expert_total = data_count * owner_count
    capacity = max(2, min(merged_count, 2 * merged_count * TOP // expert_total))
    shape = (lax.axis_size("section"), data_count, owner_count)
    if shape == (2, 4, 4) and merged_count <= 2 * capacity:
        return dense_experts(proj_own, routes, gates, w_gate, w_up, w_down)
    return routed_experts(proj_own, routes, gates, w_gate, w_up, w_down, capacity)


def solution(mesh):
    return jax.shard_map(
        per_device,
        mesh=mesh,
        in_specs=(
            P(("dp", "expert"), None),
            P(("dp", "expert"), None),
            P(None, "section"),
            P("section", None),
            P("dp", "section"),
            P(("dp", "expert"), None),
            P(("dp", "expert"), None),
            P(("dp", "expert"), None, "section"),
            P(("dp", "expert"), None, "section"),
            P(("dp", "expert"), "section", None),
        ),
        out_specs=P(("dp", "expert"), "section"),
        check_vma=False,
    )
```

```python
import math

import jax
import jax.numpy as jnp
from jax import lax
from jax.sharding import PartitionSpec as P

D_VIT = 1152
HEADS = 16
TOP = 6


def layer_norm(values):
    center = values - jnp.mean(values, axis=-1, keepdims=True)
    spread = jnp.mean(center * center, axis=-1, keepdims=True)
    return center * lax.rsqrt(spread + 1e-06)


def rms_norm(values):
    return values * lax.rsqrt(jnp.mean(values * values, axis=-1, keepdims=True) + 1e-06)


def swapped(values, axis, bit):
    count = lax.axis_size(axis)
    return lax.ppermute(values, axis, [(i, i ^ bit) for i in range(count)])


def pair_sum(own, other):
    return (own.astype(jnp.float32) + other.astype(jnp.float32)).astype(jnp.bfloat16)


def along_expert(values):
    far = jnp.stack([values, swapped(values, "expert", 2)])
    return jnp.concatenate([far, swapped(far, "expert", 1)])


def expert_weights(routes, gates):
    owners = lax.axis_size("expert")
    groups = lax.axis_size("dp") * owners
    own_expert = lax.axis_index("dp") * owners + lax.axis_index("expert")
    at_expert = jnp.arange(groups, dtype=jnp.int32)[None, :]
    per_expert = jnp.sum(
        jnp.where(routes[:, :, None] == at_expert[None], gates[:, :, None], 0.0), axis=1
    )
    found = {0: along_expert(per_expert)}
    found[2] = swapped(found[0], "dp", 2)
    for flip in (0, 2):
        found[flip + 1] = swapped(found[flip], "dp", 1)
    return {
        flip: jnp.sum(
            jnp.where(at_expert == own_expert, piece.reshape(-1, groups), 0.0),
            axis=1,
            keepdims=True,
        )
        for flip, piece in found.items()
    }


def dense_experts(proj_own, weights, w_gate, w_up, w_down):
    sections = lax.axis_size("section")
    data_count = lax.axis_size("dp")
    owners = lax.axis_size("expert")
    rows, part = proj_own.shape
    me_s = lax.axis_index("section")
    own = proj_own.astype(jnp.float32)
    squares = jnp.sum(own * own, axis=1)
    squares = squares + swapped(squares, "section", 1)
    normed = (own * lax.rsqrt(squares / (sections * part) + 1e-06)[:, None]).astype(jnp.bfloat16)
    half = part // 2
    left = {(0, 0): along_expert(normed[:, :half]).reshape(owners * rows, half)}
    right = {(0, 0): along_expert(normed[:, half:]).reshape(owners * rows, half)}
    left[0, 1] = swapped(left[0, 0], "section", 1)
    right[2, 0] = swapped(right[0, 0], "dp", 2)
    right[0, 1] = swapped(right[0, 0], "section", 1)
    left[2, 0] = swapped(left[0, 0], "dp", 2)
    left[2, 1] = swapped(left[0, 1], "dp", 2)
    right[2, 1] = swapped(right[2, 0], "section", 1)
    tokens = {}
    for flip in (0, 2):
        pieces = [side[flip, q] for q in range(sections) for side in (left, right)]
        tokens[flip] = jnp.concatenate(pieces, axis=1)
        tokens[flip + 1] = jnp.concatenate([swapped(p, "dp", 1) for p in pieces], axis=1)

    def turned(matrix):
        return jnp.concatenate(
            [
                lax.dynamic_slice_in_dim(matrix[0], (me_s ^ flip) * part, part, axis=0)
                for flip in range(sections)
            ],
            axis=0,
        )

    w_gate, w_up = turned(w_gate), turned(w_up)
    down = [
        lax.dynamic_slice_in_dim(w_down[0], (me_s ^ flip) * part, part, axis=1)
        for flip in range(sections)
    ]

    def run(flip):
        gate_act = jnp.dot(tokens[flip], w_gate, preferred_element_type=jnp.float32)
        up_act = jnp.dot(tokens[flip], w_up, preferred_element_type=jnp.float32)
        hidden = (jax.nn.silu(gate_act) * up_act).astype(jnp.bfloat16)
        return [
            (jnp.dot(hidden, piece, preferred_element_type=jnp.float32) * weights[flip]).astype(
                jnp.bfloat16
            )
            for piece in down
        ]

    partial = {flip: run(flip) for flip in range(data_count)}
    near = {}
    for flip in range(data_count - 2, -1, -2):
        near[flip] = [
            pair_sum(partial[flip][q], swapped(partial[flip + 1][q], "dp", 1))
            for q in range(sections)
        ]
    left = [piece[:, :half] for piece in near[0]], [piece[:, :half] for piece in near[2]]
    right = [piece[:, half:] for piece in near[0]], [piece[:, half:] for piece in near[2]]
    far_left = pair_sum(left[1][0], swapped(left[1][1], "section", 1))
    far_right = pair_sum(right[0][1], swapped(right[1][1], "dp", 2))
    mid_left = pair_sum(left[0][0], swapped(left[0][1], "section", 1))
    mid_right = pair_sum(right[0][0], swapped(right[1][0], "dp", 2))
    mid_left = pair_sum(mid_left, swapped(far_left, "dp", 2))
    mid_right = pair_sum(mid_right, swapped(far_right, "section", 1))
    ends = []
    for piece in (mid_left, mid_right):
        piece = piece.reshape(owners, rows, half)
        piece = pair_sum(piece[:2], swapped(piece[2:], "expert", 1))
        ends.append(
            piece[0].astype(jnp.float32) + swapped(piece[1], "expert", 2).astype(jnp.float32)
        )
    return (own + jnp.concatenate(ends, axis=1)).astype(jnp.bfloat16)


def routed_experts(proj_own, routes, gates, w_gate, w_up, w_down, capacity):
    projected = lax.all_gather(proj_own, "section", axis=1, tiled=True)
    model_width = projected.shape[1]
    normed_tokens = rms_norm(projected.astype(jnp.float32)).astype(jnp.bfloat16)
    expert_total = lax.axis_size("dp") * lax.axis_size("expert")
    merged_count = proj_own.shape[0]
    route_flat = routes.reshape(-1)
    onehot = (route_flat[:, None] == jnp.arange(expert_total, dtype=jnp.int32)[None, :]).astype(
        jnp.int32
    )
    ranks = jnp.cumsum(onehot, axis=0) - 1
    slots = jnp.sum(ranks * onehot, axis=1)
    target = route_flat * capacity + slots
    owners = jnp.arange(merged_count * TOP, dtype=jnp.int32) // TOP
    source = jnp.zeros((expert_total * capacity,), dtype=jnp.int32).at[target].set(owners)
    outgoing = normed_tokens[source].reshape(expert_total, capacity, model_width)
    received = lax.all_to_all(outgoing, ("dp", "expert"), split_axis=0, concat_axis=0, tiled=True)
    flat_rows = received.reshape(-1, received.shape[-1])
    gate_act = jnp.dot(flat_rows, w_gate[0], preferred_element_type=jnp.float32)
    up_act = jnp.dot(flat_rows, w_up[0], preferred_element_type=jnp.float32)
    hidden = (jax.nn.silu(gate_act) * up_act).astype(jnp.bfloat16)
    result = jnp.dot(hidden, w_down[0], preferred_element_type=jnp.float32).astype(jnp.bfloat16)
    returned = lax.all_to_all(
        result.reshape(received.shape[:-1] + (w_down.shape[2],)),
        ("dp", "expert"),
        split_axis=0,
        concat_axis=0,
        tiled=True,
    )
    picked = returned.reshape(expert_total * capacity, model_width)[target].reshape(
        merged_count, TOP, model_width
    )
    weighted = jnp.zeros((merged_count, model_width), dtype=jnp.float32)
    for choice_index in range(TOP):
        weighted = weighted + gates[:, choice_index : choice_index + 1] * picked[
            :, choice_index
        ].astype(jnp.float32)
    expert_cols = lax.psum_scatter(
        weighted.astype(jnp.bfloat16), "section", scatter_dimension=1, tiled=True
    ).astype(jnp.float32)
    return (proj_own.astype(jnp.float32) + expert_cols).astype(jnp.bfloat16)


def per_device(patches, lengths, w_qkv, w_out, w_proj, routes, gates, w_gate, w_up, w_down):
    data_count = lax.axis_size("dp")
    owner_count = lax.axis_size("expert")
    patch_rows, width = patches.shape
    head_dim = D_VIT // HEADS
    local_heads = w_qkv.shape[1] // (3 * head_dim)
    scale = 1.0 / math.sqrt(head_dim)
    merged_count = patch_rows // 4
    expert_total = data_count * owner_count
    capacity = max(2, min(merged_count, 2 * merged_count * TOP // expert_total))
    shape = (lax.axis_size("section"), data_count, owner_count)
    dense = shape == (2, 4, 4) and merged_count <= 2 * capacity
    weights = expert_weights(routes, gates) if dense else None
    shards = [(0, w_proj)]
    bit = data_count // 2
    while bit >= 1:
        shards = shards + [(flip ^ bit, swapped(shard, "dp", bit)) for flip, shard in shards]
        bit //= 2
    normed_in = layer_norm(patches.astype(jnp.float32)).astype(jnp.bfloat16)
    packed = jnp.dot(normed_in, w_qkv, preferred_element_type=jnp.float32).astype(jnp.bfloat16)
    packed = packed.reshape(patch_rows, local_heads, 3, head_dim)
    query = packed[:, :, 0]
    key_part = packed[:, :, 1]
    value_part = packed[:, :, 2]
    ends = jnp.cumsum(lengths[0]) * 4
    places = jnp.arange(patch_rows, dtype=jnp.int32)
    segment = jnp.sum((places[:, None] >= ends[None, :]).astype(jnp.int32), axis=1)
    block_rows = min(patch_rows, 512)
    block_count = patch_rows // block_rows

    def attend(blocks):
        query_block, segment_block = blocks
        scores = (
            jnp.einsum("qhd,khd->hqk", query_block, key_part, preferred_element_type=jnp.float32)
            * scale
        )
        same = segment_block[:, None] == segment[None, :]
        scores = jnp.where(same[None], scores, -jnp.inf)
        peak = jnp.max(scores, axis=-1, keepdims=True)
        weights = jnp.where(same[None], jnp.exp(scores - peak), 0.0)
        probs = (weights / jnp.sum(weights, axis=-1, keepdims=True)).astype(jnp.bfloat16)
        result = jnp.einsum("hqk,khd->qhd", probs, value_part, preferred_element_type=jnp.float32)
        return result.astype(jnp.bfloat16).reshape(block_rows, local_heads * head_dim)

    attended = lax.map(
        attend,
        (
            query.reshape(block_count, block_rows, local_heads, head_dim),
            segment.reshape(block_count, block_rows),
        ),
    )
    attended = attended.reshape(patch_rows, local_heads * head_dim)
    mixed = jnp.dot(attended, w_out, preferred_element_type=jnp.float32).astype(jnp.bfloat16)
    if lax.axis_size("section") == 2:
        summed = mixed.astype(jnp.float32) + swapped(mixed, "section", 1).astype(jnp.float32)
    else:
        summed = lax.psum(mixed, "section").astype(jnp.float32)
    merged = (
        (patches.astype(jnp.float32) + summed).reshape(merged_count, 4 * width).astype(jnp.bfloat16)
    )
    depth = w_proj.shape[0]
    me_d = lax.axis_index("dp")
    proj_own = sum(
        jnp.dot(
            lax.dynamic_slice_in_dim(merged, (me_d ^ flip) * depth, depth, axis=1),
            shard,
            preferred_element_type=jnp.float32,
        )
        for flip, shard in shards
    ).astype(jnp.bfloat16)
    if dense:
        return dense_experts(proj_own, weights, w_gate, w_up, w_down)
    return routed_experts(proj_own, routes, gates, w_gate, w_up, w_down, capacity)


def solution(mesh):
    return jax.shard_map(
        per_device,
        mesh=mesh,
        in_specs=(
            P(("dp", "expert"), None),
            P(("dp", "expert"), None),
            P(None, "section"),
            P("section", None),
            P("dp", "section"),
            P(("dp", "expert"), None),
            P(("dp", "expert"), None),
            P(("dp", "expert"), None, "section"),
            P(("dp", "expert"), None, "section"),
            P(("dp", "expert"), "section", None),
        ),
        out_specs=P(("dp", "expert"), "section"),
        check_vma=False,
    )
```

```python
import math

import jax
import jax.numpy as jnp
from jax import lax
from jax.sharding import PartitionSpec as P

D_VIT = 1152
HEADS = 16
TOP = 6


def layer_norm(values):
    center = values - jnp.mean(values, axis=-1, keepdims=True)
    spread = jnp.mean(center * center, axis=-1, keepdims=True)
    return center * lax.rsqrt(spread + 1e-06)


def rms_norm(values):
    return values * lax.rsqrt(jnp.mean(values * values, axis=-1, keepdims=True) + 1e-06)


def swapped(values, axis, bit):
    count = lax.axis_size(axis)
    return lax.ppermute(values, axis, [(i, i ^ bit) for i in range(count)])


def pair_sum(own, other):
    return (own.astype(jnp.float32) + other.astype(jnp.float32)).astype(jnp.bfloat16)


def along_expert(values):
    far = jnp.stack([values, swapped(values, "expert", 2)])
    return jnp.concatenate([far, swapped(far, "expert", 1)])


def expert_weights(routes, gates):
    owners = lax.axis_size("expert")
    groups = lax.axis_size("dp") * owners
    own_expert = lax.axis_index("dp") * owners + lax.axis_index("expert")
    at_expert = jnp.arange(groups, dtype=jnp.int32)[None, :]
    per_expert = jnp.sum(
        jnp.where(routes[:, :, None] == at_expert[None], gates[:, :, None], 0.0), axis=1
    )
    found = {0: along_expert(per_expert)}
    found[2] = swapped(found[0], "dp", 2)
    for flip in (0, 2):
        found[flip + 1] = swapped(found[flip], "dp", 1)
    return {
        flip: jnp.sum(
            jnp.where(at_expert == own_expert, piece.reshape(-1, groups), 0.0),
            axis=1,
            keepdims=True,
        )
        for flip, piece in found.items()
    }


def turned_weights(w_gate, w_up, w_down, part):
    me_s, sections = lax.axis_index("section"), lax.axis_size("section")
    starts = [(me_s ^ flip) * part for flip in range(sections)]

    def turned(matrix):
        return jnp.concatenate(
            [lax.dynamic_slice_in_dim(matrix[0], start, part, axis=0) for start in starts], axis=0
        )

    down = [lax.dynamic_slice_in_dim(w_down[0], start, part, axis=1) for start in starts]
    return turned(w_gate), turned(w_up), down


def dense_experts(proj_own, weights, w_gate, w_up, down):
    sections = lax.axis_size("section")
    data_count = lax.axis_size("dp")
    owners = lax.axis_size("expert")
    rows, part = proj_own.shape
    own = proj_own.astype(jnp.float32)
    squares = jnp.sum(own * own, axis=1)
    squares = squares + swapped(squares, "section", 1)
    normed = (own * lax.rsqrt(squares / (sections * part) + 1e-06)[:, None]).astype(jnp.bfloat16)
    half = part // 2
    left = {(0, 0): along_expert(normed[:, :half]).reshape(owners * rows, half)}
    right = {(0, 0): along_expert(normed[:, half:]).reshape(owners * rows, half)}
    left[0, 1] = swapped(left[0, 0], "section", 1)
    right[2, 0] = swapped(right[0, 0], "dp", 2)
    right[0, 1] = swapped(right[0, 0], "section", 1)
    left[2, 0] = swapped(left[0, 0], "dp", 2)
    left[2, 1] = swapped(left[0, 1], "dp", 2)
    right[2, 1] = swapped(right[2, 0], "section", 1)
    tokens = {}
    for flip in (0, 2):
        pieces = [side[flip, q] for q in range(sections) for side in (left, right)]
        tokens[flip] = jnp.concatenate(pieces, axis=1)
        tokens[flip + 1] = jnp.concatenate([swapped(p, "dp", 1) for p in pieces], axis=1)

    def run(flip):
        gate_act = jnp.dot(tokens[flip], w_gate, preferred_element_type=jnp.float32)
        up_act = jnp.dot(tokens[flip], w_up, preferred_element_type=jnp.float32)
        hidden = (jax.nn.silu(gate_act) * up_act).astype(jnp.bfloat16)
        return [
            (jnp.dot(hidden, piece, preferred_element_type=jnp.float32) * weights[flip]).astype(
                jnp.bfloat16
            )
            for piece in down
        ]

    partial = {flip: run(flip) for flip in range(data_count)}
    near = {}
    for flip in range(data_count - 2, -1, -2):
        near[flip] = [
            pair_sum(partial[flip][q], swapped(partial[flip + 1][q], "dp", 1))
            for q in range(sections)
        ]
    left = [piece[:, :half] for piece in near[0]], [piece[:, :half] for piece in near[2]]
    right = [piece[:, half:] for piece in near[0]], [piece[:, half:] for piece in near[2]]
    far_left = pair_sum(left[1][0], swapped(left[1][1], "section", 1))
    far_right = pair_sum(right[0][1], swapped(right[1][1], "dp", 2))
    mid_left = pair_sum(left[0][0], swapped(left[0][1], "section", 1))
    mid_right = pair_sum(right[0][0], swapped(right[1][0], "dp", 2))
    mid_left = pair_sum(mid_left, swapped(far_left, "dp", 2))
    mid_right = pair_sum(mid_right, swapped(far_right, "section", 1))
    ends = []
    for piece in (mid_left, mid_right):
        piece = piece.reshape(owners, rows, half)
        piece = pair_sum(piece[:2], swapped(piece[2:], "expert", 1))
        ends.append(
            piece[0].astype(jnp.float32) + swapped(piece[1], "expert", 2).astype(jnp.float32)
        )
    return (own + jnp.concatenate(ends, axis=1)).astype(jnp.bfloat16)


def routed_experts(proj_own, routes, gates, w_gate, w_up, w_down, capacity):
    projected = lax.all_gather(proj_own, "section", axis=1, tiled=True)
    model_width = projected.shape[1]
    normed_tokens = rms_norm(projected.astype(jnp.float32)).astype(jnp.bfloat16)
    expert_total = lax.axis_size("dp") * lax.axis_size("expert")
    merged_count = proj_own.shape[0]
    route_flat = routes.reshape(-1)
    onehot = (route_flat[:, None] == jnp.arange(expert_total, dtype=jnp.int32)[None, :]).astype(
        jnp.int32
    )
    ranks = jnp.cumsum(onehot, axis=0) - 1
    slots = jnp.sum(ranks * onehot, axis=1)
    target = route_flat * capacity + slots
    owners = jnp.arange(merged_count * TOP, dtype=jnp.int32) // TOP
    source = jnp.zeros((expert_total * capacity,), dtype=jnp.int32).at[target].set(owners)
    outgoing = normed_tokens[source].reshape(expert_total, capacity, model_width)
    received = lax.all_to_all(outgoing, ("dp", "expert"), split_axis=0, concat_axis=0, tiled=True)
    flat_rows = received.reshape(-1, received.shape[-1])
    gate_act = jnp.dot(flat_rows, w_gate[0], preferred_element_type=jnp.float32)
    up_act = jnp.dot(flat_rows, w_up[0], preferred_element_type=jnp.float32)
    hidden = (jax.nn.silu(gate_act) * up_act).astype(jnp.bfloat16)
    result = jnp.dot(hidden, w_down[0], preferred_element_type=jnp.float32).astype(jnp.bfloat16)
    returned = lax.all_to_all(
        result.reshape(received.shape[:-1] + (w_down.shape[2],)),
        ("dp", "expert"),
        split_axis=0,
        concat_axis=0,
        tiled=True,
    )
    picked = returned.reshape(expert_total * capacity, model_width)[target].reshape(
        merged_count, TOP, model_width
    )
    weighted = jnp.zeros((merged_count, model_width), dtype=jnp.float32)
    for choice_index in range(TOP):
        weighted = weighted + gates[:, choice_index : choice_index + 1] * picked[
            :, choice_index
        ].astype(jnp.float32)
    expert_cols = lax.psum_scatter(
        weighted.astype(jnp.bfloat16), "section", scatter_dimension=1, tiled=True
    ).astype(jnp.float32)
    return (proj_own.astype(jnp.float32) + expert_cols).astype(jnp.bfloat16)


def per_device(patches, lengths, w_qkv, w_out, w_proj, routes, gates, w_gate, w_up, w_down):
    data_count = lax.axis_size("dp")
    owner_count = lax.axis_size("expert")
    patch_rows, width = patches.shape
    head_dim = D_VIT // HEADS
    local_heads = w_qkv.shape[1] // (3 * head_dim)
    scale = 1.0 / math.sqrt(head_dim)
    merged_count = patch_rows // 4
    expert_total = data_count * owner_count
    capacity = max(2, min(merged_count, 2 * merged_count * TOP // expert_total))
    shape = (lax.axis_size("section"), data_count, owner_count)
    dense = shape == (2, 4, 4) and merged_count <= 2 * capacity
    weights = expert_weights(routes, gates) if dense else None
    shards = [(0, w_proj)]
    bit = data_count // 2
    while bit >= 1:
        shards = shards + [(flip ^ bit, swapped(shard, "dp", bit)) for flip, shard in shards]
        bit //= 2
    normed_in = layer_norm(patches.astype(jnp.float32)).astype(jnp.bfloat16)
    packed = jnp.dot(normed_in, w_qkv, preferred_element_type=jnp.float32).astype(jnp.bfloat16)
    packed = packed.reshape(patch_rows, local_heads, 3, head_dim)
    query = packed[:, :, 0]
    key_part = packed[:, :, 1]
    value_part = packed[:, :, 2]
    ends = jnp.cumsum(lengths[0]) * 4
    places = jnp.arange(patch_rows, dtype=jnp.int32)
    segment = jnp.sum((places[:, None] >= ends[None, :]).astype(jnp.int32), axis=1)
    block_rows = min(patch_rows, 512)
    block_count = patch_rows // block_rows

    def attend(blocks):
        query_block, segment_block = blocks
        scores = (
            jnp.einsum("qhd,khd->hqk", query_block, key_part, preferred_element_type=jnp.float32)
            * scale
        )
        same = segment_block[:, None] == segment[None, :]
        scores = jnp.where(same[None], scores, -jnp.inf)
        peak = jnp.max(scores, axis=-1, keepdims=True)
        weights = jnp.where(same[None], jnp.exp(scores - peak), 0.0)
        probs = (weights / jnp.sum(weights, axis=-1, keepdims=True)).astype(jnp.bfloat16)
        result = jnp.einsum("hqk,khd->qhd", probs, value_part, preferred_element_type=jnp.float32)
        return result.astype(jnp.bfloat16).reshape(block_rows, local_heads * head_dim)

    attended = lax.map(
        attend,
        (
            query.reshape(block_count, block_rows, local_heads, head_dim),
            segment.reshape(block_count, block_rows),
        ),
    )
    attended = attended.reshape(patch_rows, local_heads * head_dim)
    mixed = jnp.dot(attended, w_out, preferred_element_type=jnp.float32).astype(jnp.bfloat16)
    if lax.axis_size("section") == 2:
        other = swapped(mixed, "section", 1)
        if dense:
            matrices = turned_weights(w_gate, w_up, w_down, w_proj.shape[1])
            other, weights, matrices = lax.optimization_barrier((other, weights, matrices))
        summed = mixed.astype(jnp.float32) + other.astype(jnp.float32)
    else:
        summed = lax.psum(mixed, "section").astype(jnp.float32)
    merged = (
        (patches.astype(jnp.float32) + summed).reshape(merged_count, 4 * width).astype(jnp.bfloat16)
    )
    depth = w_proj.shape[0]
    me_d = lax.axis_index("dp")
    proj_own = sum(
        jnp.dot(
            lax.dynamic_slice_in_dim(merged, (me_d ^ flip) * depth, depth, axis=1),
            shard,
            preferred_element_type=jnp.float32,
        )
        for flip, shard in shards
    ).astype(jnp.bfloat16)
    if dense:
        return dense_experts(proj_own, weights, *matrices)
    return routed_experts(proj_own, routes, gates, w_gate, w_up, w_down, capacity)


def solution(mesh):
    return jax.shard_map(
        per_device,
        mesh=mesh,
        in_specs=(
            P(("dp", "expert"), None),
            P(("dp", "expert"), None),
            P(None, "section"),
            P("section", None),
            P("dp", "section"),
            P(("dp", "expert"), None),
            P(("dp", "expert"), None),
            P(("dp", "expert"), None, "section"),
            P(("dp", "expert"), None, "section"),
            P(("dp", "expert"), "section", None),
        ),
        out_specs=P(("dp", "expert"), "section"),
        check_vma=False,
    )
```
